512 devices in a mesh: dp: 16 (over y, x), expert: 32 (over z, core).
Axes of the slice: x: 4, y: 4, z: 16, core: 2. Of those that a mesh axis runs over, the one named last changes fastest.
Arguments:
- cotangent: bfloat16 [65536, 2048], P(('dp', 'expert')), may hold values from -0.375 to 0.375
- routes: int32 [65536, 8], P(('dp', 'expert')), may hold values from 0 to 63, all different within a row; in each aligned block of 128 rows (0 to 127, 128 to 255, ...) at most 20 rows name the same one
- gate_weights: float32 [65536, 8], P(('dp', 'expert')), may hold values from 0.05 to 0.25
- hidden: bfloat16 [16, 64, 640, 768], P('dp', 'expert'), may hold values from -6 to 6
- galore_basis: bfloat16 [64, 768, 256], P('expert'), may hold values from -0.21875 to 0.21875
- moment: float32 [64, 256, 2048], P('expert', None, 'dp'), may hold values from -1.75 to 1.75
- second: float32 [64, 256, 2048], P('expert', None, 'dp'), may hold values from 0.01 to 1
Outputs:
- new_moment: float32 [64, 256, 2048], P('expert', None, 'dp')
- new_second: float32 [64, 256, 2048], P('expert', None, 'dp')
- update: float32 [64, 256, 2048], P('expert', None, 'dp')
The draws below stay inside these ranges and needn't reach their ends.
Inputs may be any that keep to these rules, and one draw needn't show every extreme that they name: `routes`: in the rows of one device (128 aligned rows) no expert is named by more than 20 rows, a bound that some blocks reach.
All inputs are finite; a program needn't handle non-finite values.
Results may differ from the reference program's by a relative error of at most 0.0015.
Values may be sent and summed in bfloat16 or wider, within the bound.
A program may use at most 64 MiB of HBM per device.

```python
import math
import jax
import jax.numpy as jnp
import numpy as np
from jax import lax

D = 2048
F = 768
R = 256
TOPK = 8
EXP_DEV = 2
STEP = 100
TOK_DEV = 128
EXPERTS = 64
CAP = 20
SLOTS = 640
TOKENS = 65536
N_DP = 16
N_EXPERT = 32


def levels(stream_key, dims, split, low, largest):
    gain, own = 1.0, jax.random.fold_in(stream_key, 6)
    for position, blocks in split:
        steps = jnp.exp(jax.random.uniform(jax.random.fold_in(own, position), (blocks,), jnp.float32, low / len(split), largest / len(split)))
        gain = gain * jnp.repeat(steps, dims[position] // blocks).reshape([-1 if axis == position else 1 for axis in range(len(dims))])
    return gain


def assign_block(stream_key, own, number, rows, amount, top, reach, lean):
    order = jax.random.permutation(stream_key, amount)
    packed, ordinary = portions_of(amount, rows * top, reach, lean, True), portions_of(amount, rows * top, reach, lean, False)
    places = jnp.arange(amount)

    def named(tallies, offset_by):
        used = int((tallies > 0).sum())
        fixed = max(1, used // 4)
        moved = fixed + (places - fixed + offset_by * (used - fixed)) % max(1, amount - fixed)
        return jnp.zeros((amount,), jnp.int32).at[order[jnp.where(places < fixed, places, moved)]].set(jnp.asarray(tallies, jnp.int32))

    tallies = jnp.where(number % 4 == 0, named(packed, number // 4), named(ordinary, number - number // 4 - 1))
    mixed = jax.random.permutation(jax.random.fold_in(own, 3), amount)
    donor, receiver = mixed[0:amount // 2 * 2:2], mixed[1:amount // 2 * 2:2]
    margin = jnp.minimum(tallies[donor] - 1, reach - tallies[receiver]) // 2
    margin = jnp.where((donor == order[0]) | (receiver == order[0]) | (tallies[receiver] == 0), 0, jnp.maximum(margin, 0))
    moved = jax.random.randint(jax.random.fold_in(own, 4), (amount // 2,), 0, 1 << 20) % (margin + 1)
    tallies = tallies.at[donor].add(-moved).at[receiver].add(moved)
    labels = jnp.searchsorted(jnp.cumsum(tallies), jnp.arange(rows * top), side="right").astype(jnp.int32)
    table = labels.reshape(top, rows).T
    table = table[jax.random.permutation(jax.random.fold_in(own, 1), rows)]
    offset_by = jax.random.randint(jax.random.fold_in(own, 2), (rows, 1), 0, top)
    return jnp.take_along_axis(table, (jnp.arange(top)[None, :] + offset_by) % top, axis=1)


def portions_of(amount, total, limit, skew, full):
    loads = [(1 << 20) // math.isqrt(rank ** skew) + 1 for rank in range(1, amount + 1)]
    largest = limit if full else min(limit, max(-(-total // amount), total * loads[0] // sum(loads)))
    least = 1 if total - largest >= amount - 1 else 0
    given, surplus = [largest] + [least] * (amount - 1), total - largest - least * (amount - 1)
    while surplus > 0:
        free = [i for i in range(1, amount) if given[i] < largest] or [i for i in range(1, amount) if given[i] < limit]
        mass, remaining = sum([loads[i] for i in free]), surplus
        for i in free:
            extra = min(limit - given[i], max(1, remaining * loads[i] // mass), surplus)
            given[i] = given[i] + extra
            surplus = surplus - extra
    return np.array(given)


def bell_draw(stream_key, dims, spread, bound, pieces=(), held_as=jnp.bfloat16):
    values = jax.random.normal(stream_key, dims, jnp.float32) * spread
    if len(pieces) > 0:
        values = levels(stream_key, dims, pieces, -0.22, 0.18) * values
    return jnp.clip(values, min=-bound, max=bound).astype(held_as)


def setup_inputs(seed: int = 0) -> dict:
    key_of = jax.random.split(jax.random.key(seed), 8)
    cotangent = bell_draw(key_of[0], (TOKENS, D), (6.0 / (TOK_DEV * TOPK * N_DP // EXP_DEV) ** 0.5), 0.375, ((0, 512),))
    routes_keys = jax.random.split(jax.random.fold_in(key_of[1], 1), TOKENS // TOK_DEV)
    routes_turns = jax.random.permutation(jax.random.fold_in(key_of[1], 3), TOKENS // TOK_DEV)
    routes = jax.vmap(lambda own, number: assign_block(jax.random.fold_in(key_of[1], 2), own, number, TOK_DEV, EXPERTS, TOPK, CAP, 2))(routes_keys, routes_turns).reshape((TOKENS, TOPK))
    gate_weights = jnp.clip(0.05 + 0.2 * jax.random.uniform(key_of[2], (TOKENS, TOPK), jnp.float32) ** levels(key_of[2], (TOKENS, TOPK), ((0, 512),), -0.2, 0.2), 0.05, 0.25)
    hidden = bell_draw(key_of[3], (N_DP, EXPERTS, SLOTS, F), 1.0, 6.0, ((0, 16), (1, 32)))
    galore_basis = bell_draw(key_of[4], (EXPERTS, F, R), F ** -0.5, 0.21875, ((0, 32),))
    moment = bell_draw(key_of[5], (EXPERTS, R, D), 0.3, 1.75, ((0, 32), (2, 16)), jnp.float32)
    second = jnp.clip(jnp.exp(math.log(1.0) - 4.6051702 * jax.random.uniform(key_of[6], (EXPERTS, R, D), jnp.float32) ** levels(key_of[6], (EXPERTS, R, D), ((0, 32), (2, 16)), -0.2, 0.2)), 0.01, 1.0)
    return {"cotangent": cotangent, "routes": routes, "gate_weights": gate_weights, "hidden": hidden, "galore_basis": galore_basis, "moment": moment, "second": second}


beta_one = 0.9
beta_two = 0.999
epsilon = 1e-08

def route_slots(flat_routes, experts):
    onehot = (flat_routes[:, None] == jnp.arange(experts, dtype=jnp.int32)[None, :]).astype(jnp.int32)
    before = jnp.cumsum(onehot, axis=0) - onehot
    return lax.optimization_barrier(jnp.sum(before * onehot, axis=1))

def expert_grad(operands):
    hidden_rows, basis_block, table_block = operands
    projected = jnp.dot(hidden_rows, basis_block, preferred_element_type=jnp.float32).astype(jnp.bfloat16)
    return jnp.dot(projected.T, table_block, preferred_element_type=jnp.float32)

def reference(cotangent, routes, gate_weights, hidden, galore_basis, moment, second):
    experts = galore_basis.shape[0]
    replica_tokens = TOK_DEV * N_EXPERT
    route_total = TOK_DEV * TOPK
    senders = jnp.arange(N_EXPERT, dtype=jnp.int32)

    def replica(total, replica_index):
        offset = replica_index * replica_tokens
        cot_block = lax.dynamic_slice_in_dim(cotangent, offset, replica_tokens, 0)
        route_block = lax.dynamic_slice_in_dim(routes, offset, replica_tokens, 0)
        gate_block = lax.dynamic_slice_in_dim(gate_weights, offset, replica_tokens, 0)
        hidden_block = lax.dynamic_index_in_dim(hidden, replica_index, 0, keepdims=False)
        flat_routes = route_block.reshape(N_EXPERT, route_total)
        slots = jax.vmap(route_slots, in_axes=(0, None))(flat_routes, experts)
        target = (senders[:, None] * CAP + slots).reshape(-1)
        scaled = (gate_block[:, :, None] * cot_block[:, None, :].astype(jnp.float32)).astype(jnp.bfloat16)
        table = jnp.zeros((experts, SLOTS, D), jnp.bfloat16)
        table = table.at[flat_routes.reshape(-1), target].set(scaled.reshape(-1, D))
        return (total + lax.map(expert_grad, (hidden_block, galore_basis, table)), None)
    gradient, _ = lax.scan(replica, jnp.zeros((experts, R, D), jnp.float32), jnp.arange(N_DP, dtype=jnp.int32))
    new_moment = beta_one * moment + (1.0 - beta_one) * gradient
    new_second = beta_two * second + (1.0 - beta_two) * gradient * gradient
    update = new_moment / (1.0 - beta_one ** STEP) / (jnp.sqrt(new_second / (1.0 - beta_two ** STEP)) + epsilon)
    return (new_moment, new_second, update)
```

```python
import jax
import jax.numpy as jnp
from jax import lax
from jax.sharding import PartitionSpec as P

STEP = 100


beta_one = 0.9
beta_two = 0.999
epsilon = 1e-08


def body(cotangent, routes, gate_weights, hidden, galore_basis, moment, second):
    senders = lax.axis_size("expert")
    local_experts = galore_basis.shape[0]
    capacity = hidden.shape[2] // senders
    tokens, feature_width = cotangent.shape
    me = lax.axis_index("expert")
    gathered = lax.all_gather(cotangent, "expert", axis=0)
    all_routes = lax.all_gather(routes, "expert", axis=0)
    all_gates = lax.all_gather(gate_weights, "expert", axis=0)
    projected = jnp.einsum(
        "jsf,jfr->jsr", hidden[0], galore_basis, preferred_element_type=jnp.float32
    ).astype(jnp.bfloat16)
    projected = projected.reshape(local_experts, senders, capacity, projected.shape[2])
    mine = me * local_experts + jnp.arange(local_experts, dtype=jnp.int32)
    named = all_routes[None] == mine[:, None, None, None]
    hit = jnp.any(named, axis=3)
    weight = jnp.sum(jnp.where(named, all_gates[None], 0.0), axis=3)
    earlier = jnp.tril(jnp.ones((tokens, tokens), jnp.bfloat16), -1)
    slot = jnp.einsum(
        "jsu,tu->jst", hit.astype(jnp.bfloat16), earlier, preferred_element_type=jnp.float32
    ).astype(jnp.int32)
    chosen = hit[:, :, None, :] & (
        slot[:, :, None, :] == jnp.arange(capacity, dtype=jnp.int32)[None, None, :, None]
    )
    row_weight = jnp.sum(jnp.where(chosen, weight[:, :, None, :], 0.0), axis=3)
    rows = jnp.einsum(
        "jsct,std->jscd", chosen.astype(jnp.bfloat16), gathered, preferred_element_type=jnp.float32
    )
    table = (row_weight[..., None] * rows).astype(jnp.bfloat16)
    partial_value = jnp.einsum("jscr,jscd->jrd", projected, table, preferred_element_type=jnp.float32)
    gradient = lax.psum_scatter(partial_value, "dp", scatter_dimension=2, tiled=True)
    new_moment = beta_one * moment + (1.0 - beta_one) * gradient
    new_second = beta_two * second + (1.0 - beta_two) * gradient * gradient
    update = (
        new_moment
        / (1.0 - beta_one**STEP)
        / (jnp.sqrt(new_second / (1.0 - beta_two**STEP)) + epsilon)
    )
    return (new_moment, new_second, update)


def solution(mesh):
    placed = (
        P(("dp", "expert"), None),
        P(("dp", "expert"), None),
        P(("dp", "expert"), None),
        P("dp", "expert", None, None),
        P("expert", None, None),
        P("expert", None, "dp"),
        P("expert", None, "dp"),
    )
    return jax.shard_map(
        body,
        mesh=mesh,
        in_specs=placed,
        out_specs=(P("expert", None, "dp"), P("expert", None, "dp"), P("expert", None, "dp")),
        check_vma=False,
    )
```

```python
import functools

import jax
import jax.numpy as jnp
from jax import lax
from jax.experimental import pallas as pl
from jax.experimental.pallas import tpu as pltpu
from jax.sharding import PartitionSpec as P

STEP = 100
MESH = pl.DeviceIdType.MESH

beta_one = 0.9
beta_two = 0.999
epsilon = 1e-08

NX = 4
NZ = 16
PLANE = NX * NX
HALF = 8
CAP = 20
PAIR = 2 * CAP
R = 256
LANE = 128
TOK = 128
WIDE = NX * LANE
FULL = 32767.0


def landed(ref, sem):
    pltpu.make_async_copy(ref, ref, sem).wait()


def kernel(
    cx, aux, pz, out,
    prx, pg, crx, arx, tab, gacc, rxq, rxs, txq, txs, finq, fins,
    z_send, prx_sem, c_send, a_send, c_recv, a_recv,
    sc_send, sa_send, sc_recv, sa_recv, p_send, p_recv,
    q_send, s_send, q_recv, s_recv, fq_send, fs_send, fq_recv, fs_recv,
):
    dp = lax.axis_index("dp")
    ex = lax.axis_index("expert")
    x, y = lax.rem(dp, NX), dp // NX
    z, k = ex // 2, lax.rem(ex, 2)
    sibling = z * 2 + 1 - k

    def push(src, dst, send, recv, device):
        pltpu.make_async_remote_copy(
            src_ref=src, dst_ref=dst, send_sem=send, recv_sem=recv, device_id=device, device_id_type=MESH
        ).start()

    mine = pl.ds(k * 2, 2)
    for d in range(HALF, 0, -1):
        down = lax.rem(z - d + NZ, NZ)
        push(pz.at[down], prx.at[HALF - d, mine], z_send.at[HALF - d], prx_sem.at[HALF - d, k], (dp, down * 2))
        if d < HALF:
            up = lax.rem(z + d, NZ)
            push(pz.at[up], prx.at[HALF - 1 - d, mine], z_send.at[HALF + d], prx_sem.at[HALF - 1 - d, k], (dp, up * 2 + 1))

    @pl.when(k == 0)
    def _():
        push(pz.at[z], prx.at[HALF - 1, mine], z_send.at[HALF], prx_sem.at[HALF - 1, k], (dp, sibling))

    @pl.when(k == 1)
    def _():
        pltpu.make_async_copy(pz.at[z], prx.at[HALF - 1, mine], prx_sem.at[HALF - 1, k]).start()

    pltpu.make_async_copy(cx.at[x], crx.at[dp, k], c_recv.at[dp]).start()
    pltpu.make_async_copy(aux.at[y], arx.at[dp, k], a_recv.at[dp]).start()

    def scatter(o, carry):
        to = lax.rem(dp + o, PLANE)
        push(aux.at[to // NX], arx.at[dp, k], a_send.at[o], a_recv.at[dp], (to, ex))
        push(cx.at[lax.rem(to, NX)], crx.at[dp, k], c_send.at[o], c_recv.at[dp], (to, ex))
        return carry

    lax.fori_loop(1, PLANE, scatter, 0)

    def spread(i):
        for core in range(2):
            landed(prx.at[i, pl.ds(core * 2, 2)], prx_sem.at[i, core])
        pltpu.make_async_copy(prx.at[i, y], pg.at[i, dp], p_recv.at[i]).start()

        def one(o, carry):
            to = lax.rem(dp + o, PLANE)
            push(prx.at[i, to // NX], pg.at[i, dp], p_send.at[i], p_recv.at[i], (to, ex))
            return carry

        lax.fori_loop(1, PLANE, one, 0)

    def share(o, carry):
        source = lax.rem(dp - o + PLANE, PLANE)
        landed(arx.at[source, k], a_recv.at[source])
        push(arx.at[source, k], arx.at[source, k], sa_send.at[source], sa_recv.at[source], (dp, sibling))
        landed(crx.at[source, k], c_recv.at[source])
        push(crx.at[source, k], crx.at[source, k], sc_send.at[source], sc_recv.at[source], (dp, sibling))
        return carry

    lax.fori_loop(0, 5, share, 0)
    spread(0)
    lax.fori_loop(5, 9, share, 0)
    spread(1)
    lax.fori_loop(9, 13, share, 0)
    spread(2)
    lax.fori_loop(13, PLANE, share, 0)

    first = pl.multiple_of((1 - k) * HALF, HALF)
    slot = lax.broadcasted_iota(jnp.int32, (HALF, PAIR, 2 * TOK), 1).astype(jnp.float32)

    def rows_of(r):
        landed(arx.at[r, 1 - k], sa_recv.at[r])
        landed(crx.at[r, 1 - k], sc_recv.at[r])
        place = jnp.concatenate([arx[r, c, 0, pl.ds(first, HALF), :] for c in range(2)], axis=1)
        gate = jnp.concatenate([arx[r, c, 1, pl.ds(first, HALF), :] for c in range(2)], axis=1)
        here = slot == place[:, None, :]
        weight = jnp.sum(jnp.where(here, gate[:, None, :], 0.0), axis=2, keepdims=True)
        pick = jnp.where(here, 1.0, 0.0).reshape(HALF * PAIR, 2 * TOK).astype(jnp.bfloat16)
        rows = jnp.dot(pick, crx[r].reshape(2 * TOK, WIDE), preferred_element_type=jnp.float32)
        return rows.reshape(HALF, PAIR, WIDE) * weight

    def build(pair, carry):
        both = jnp.concatenate([rows_of(2 * pair), rows_of(2 * pair + 1)], axis=1)
        tab[:, pair] = both.astype(jnp.bfloat16)
        return carry

    lax.fori_loop(0, PLANE // 2, build, 0)

    onward = lax.rem(z + 1 - 2 * k + NZ, NZ) * 2 + k

    def contribution(i):
        landed(pg.at[i], p_recv.at[i])
        got = pg[i].astype(jnp.float32).reshape(PLANE, 2, PAIR, LANE)
        projected = jnp.concatenate([got[:, h].reshape(PLANE * PAIR, LANE) for h in range(2)], axis=1)
        table = tab[jnp.where(k == 0, HALF - 1 - i, i)].reshape(PLANE * PAIR, WIDE)
        gacc[...] = lax.dot_general(
            projected.astype(jnp.bfloat16), table, (((0,), (0,)), ((), ())), preferred_element_type=jnp.float32
        )

    def arrived(i, b):
        landed(rxs.at[i, b], s_recv.at[i, b])
        landed(rxq.at[i, b], q_recv.at[i, b])
        return rxq[i, b].astype(jnp.int32).astype(jnp.float32) * rxs[i, b, 0:1, :]

    def code(value, i, b):
        most = jnp.maximum(jnp.max(jnp.abs(value), axis=0, keepdims=True), 1e-33)
        txq[i, b] = jnp.round(value * (FULL / most)).astype(jnp.int32).astype(jnp.int16)
        txs[i, b] = jnp.broadcast_to(most * (1.0 / FULL), (8, LANE))

    def block(b):
        return gacc[:, b * LANE : (b + 1) * LANE]

    def send_on(value, i, b):
        code(value, i, b)
        push(txs.at[i, b], rxs.at[i + 1, b], s_send.at[i, b], s_recv.at[i + 1, b], (dp, onward))
        push(txq.at[i, b], rxq.at[i + 1, b], q_send.at[i, b], q_recv.at[i + 1, b], (dp, onward))

    for i in range(HALF - 1):
        if i + 3 < HALF:
            spread(i + 3)
        contribution(i)
        for b in range(NX):
            send_on(block(b) if i == 0 else block(b) + arrived(i, b), i, b)
    contribution(HALF - 1)

    owner_core = y // 2
    owner = z * 2 + owner_core
    part = lax.rem(y, 2)

    def finish(value, b):
        code(value, HALF, b)
        here = (y == b) & (owner_core == k)
        to = b * NX + x

        @pl.when(here)
        def _():
            pltpu.make_async_copy(txs.at[HALF, b], fins.at[k, part], fs_recv.at[k, part]).start()
            pltpu.make_async_copy(txq.at[HALF, b], finq.at[k, part], fq_recv.at[k, part]).start()

        @pl.when(jnp.logical_not(here))
        def _():
            push(txs.at[HALF, b], fins.at[k, part], fs_send.at[b], fs_recv.at[k, part], (to, owner))
            push(txq.at[HALF, b], finq.at[k, part], fq_send.at[b], fq_recv.at[k, part], (to, owner))

    @pl.when(k == 0)
    def _():
        for b in range(NX):
            send_on(block(b) + arrived(HALF - 1, b), HALF - 1, b)
        for b in range(NX):
            finish(arrived(HALF, b), b)

    @pl.when(k == 1)
    def _():
        for b in range(NX):
            finish(block(b) + arrived(HALF - 1, b), b)

    for j in range(2):
        total = None
        for core in range(2):
            landed(fins.at[core, j], fs_recv.at[core, j])
            landed(finq.at[core, j], fq_recv.at[core, j])
            value = finq[core, j].astype(jnp.int32).astype(jnp.float32) * fins[core, j, 0:1, :]
            total = value if total is None else total + value
        out[j] = total

    for i in range(HALF):
        landed(pz.at[0], z_send.at[i])
        if i > 0:
            landed(pz.at[0], z_send.at[HALF + i])
        landed(pg.at[i, pl.ds(0, PLANE - 1)], p_send.at[i])

    @pl.when(k == 0)
    def _():
        landed(pz.at[0], z_send.at[HALF])

    def left(o, carry):
        landed(aux.at[0], a_send.at[o])
        landed(cx.at[0], c_send.at[o])
        return carry

    lax.fori_loop(1, PLANE, left, 0)

    def shared(o, carry):
        landed(aux.at[0], sa_send.at[o])
        landed(cx.at[0], sc_send.at[o])
        return carry

    lax.fori_loop(0, PLANE, shared, 0)

    def sent(i):
        for b in range(NX):
            landed(txs.at[i, b], s_send.at[i, b])
            landed(txq.at[i, b], q_send.at[i, b])

    for i in range(HALF - 1):
        sent(i)

    @pl.when(k == 0)
    def _():
        sent(HALF - 1)

    for b in range(NX):

        @pl.when(jnp.logical_not((y == b) & (owner_core == k)))
        def _():
            landed(txs.at[HALF, b], fs_send.at[b])
            landed(txq.at[HALF, b], fq_send.at[b])


def exchange(cx, aux, pz):
    dma = pltpu.SemaphoreType.DMA
    return pl.pallas_call(
        kernel,
        out_shape=jax.ShapeDtypeStruct((2, R, LANE), jnp.float32),
        in_specs=[pl.BlockSpec(memory_space=pltpu.VMEM)] * 3,
        out_specs=pl.BlockSpec(memory_space=pltpu.VMEM),
        scratch_shapes=[
            pltpu.VMEM((HALF, NX, 2 * PAIR, LANE), jnp.bfloat16),
            pltpu.VMEM((HALF, PLANE, 2 * PAIR, LANE), jnp.bfloat16),
            pltpu.VMEM((PLANE, 2, TOK, WIDE), jnp.bfloat16),
            pltpu.VMEM((PLANE, 2, 2, NZ, TOK), jnp.float32),
            pltpu.VMEM((HALF, PLANE // 2, 2 * PAIR, WIDE), jnp.bfloat16),
            pltpu.VMEM((R, WIDE), jnp.float32),
            pltpu.VMEM((HALF + 1, NX, R, LANE), jnp.int16),
            pltpu.VMEM((HALF + 1, NX, 8, LANE), jnp.float32),
            pltpu.VMEM((HALF + 1, NX, R, LANE), jnp.int16),
            pltpu.VMEM((HALF + 1, NX, 8, LANE), jnp.float32),
            pltpu.VMEM((2, 2, R, LANE), jnp.int16),
            pltpu.VMEM((2, 2, 8, LANE), jnp.float32),
            dma((2 * HALF,)),
            dma((HALF, 2)),
            dma((PLANE,)), dma((PLANE,)), dma((PLANE,)), dma((PLANE,)),
            dma((PLANE,)), dma((PLANE,)), dma((PLANE,)), dma((PLANE,)),
            dma((HALF,)), dma((HALF,)),
            dma((HALF, NX)), dma((HALF, NX)),
            dma((HALF + 1, NX)), dma((HALF + 1, NX)),
            dma((NX,)), dma((NX,)),
            dma((2, 2)), dma((2, 2)),
        ],
        compiler_params=pltpu.CompilerParams(has_side_effects=True, vmem_limit_bytes=48 * 1024 * 1024),
        cost_estimate=pl.CostEstimate(flops=2_700_000_000, bytes_accessed=4_000_000, transcendentals=0),
    )(cx, aux, pz)


def body(cotangent, routes, gate_weights, hidden, galore_basis, moment, second):
    ex = lax.axis_index("expert")
    z, k = ex // 2, ex % 2
    experts = NZ * NX
    named = routes.T[None] == jnp.arange(experts, dtype=jnp.int32)[:, None, None]
    hit = jnp.any(named, axis=1)
    gate = jnp.sum(jnp.where(named, gate_weights.T[None], 0.0), axis=1)
    earlier = jnp.triu(jnp.ones((TOK, TOK), jnp.bfloat16), 1)
    before = jnp.dot(hit.astype(jnp.bfloat16), earlier, preferred_element_type=jnp.float32)
    place = jnp.where(hit, before + (CAP * k).astype(jnp.float32), -1.0)
    aux = jnp.stack([place, gate]).reshape(2, NZ, NX, TOK)
    aux = jnp.roll(aux, 7 - z, axis=1).transpose(2, 0, 1, 3)
    cx = cotangent.reshape(TOK, NX, NX, LANE).transpose(2, 0, 1, 3).reshape(NX, TOK, WIDE)
    projected = jnp.einsum(
        "jsf,jfr->jsr", hidden[0], galore_basis, preferred_element_type=jnp.float32
    ).astype(jnp.bfloat16)
    pz = projected.reshape(2, NZ, PAIR, 2, LANE).transpose(1, 0, 3, 2, 4).reshape(NZ, 2, 2 * PAIR, LANE)
    gradient = exchange(cx, aux, pz)
    new_moment = beta_one * moment + (1.0 - beta_one) * gradient
    new_second = beta_two * second + (1.0 - beta_two) * gradient * gradient
    update = (
        new_moment
        / (1.0 - beta_one**STEP)
        / (jnp.sqrt(new_second / (1.0 - beta_two**STEP)) + epsilon)
    )
    return (new_moment, new_second, update)


def solution(mesh):
    placed = (
        P(("dp", "expert"), None),
        P(("dp", "expert"), None),
        P(("dp", "expert"), None),
        P("dp", "expert", None, None),
        P("expert", None, None),
        P("expert", None, "dp"),
        P("expert", None, "dp"),
    )
    return jax.shard_map(
        body,
        mesh=mesh,
        in_specs=placed,
        out_specs=(P("expert", None, "dp"), P("expert", None, "dp"), P("expert", None, "dp")),
        check_vma=False,
    )
```

```python
import functools

import jax
import jax.numpy as jnp
from jax import lax
from jax.experimental import pallas as pl
from jax.experimental.pallas import tpu as pltpu
from jax.sharding import PartitionSpec as P

STEP = 100
MESH = pl.DeviceIdType.MESH

beta_one = 0.9
beta_two = 0.999
epsilon = 1e-08

NX = 4
NZ = 16
PLANE = NX * NX
HALF = 8
CAP = 20
PAIR = 2 * CAP
R = 256
LANE = 128
TOK = 128
WIDE = NX * LANE
FULL = 32767.0


def landed(ref, sem):
    pltpu.make_async_copy(ref, ref, sem).wait()


def kernel(
    cot, routes_in, gates_in, hidden, basis, out,
    routes, gates, cx, aux, hid, bas, pz, load_sem, prx, pg, crx, arx, tab, pt, own, rxq, rxs, txq, txs, finq, fins,
    z_send, prx_sem, c_send, a_send, c_recv, a_recv, cy_send, ax_send,
    sc_send, sa_send, sc_recv, sa_recv, p1_send, p1_recv, p2_send, p2_recv,
    q_send, s_send, q_recv, s_recv, fq_recv, fs_recv,
):
    dp = lax.axis_index("dp")
    ex = lax.axis_index("expert")
    x, y = lax.rem(dp, NX), dp // NX
    z, k = ex // 2, lax.rem(ex, 2)
    sibling = z * 2 + 1 - k
    ahead = 1 - 2 * k

    def push(src, dst, send, recv, device):
        pltpu.make_async_remote_copy(
            src_ref=src, dst_ref=dst, send_sem=send, recv_sem=recv, device_id=device, device_id_type=MESH
        ).start()

    def chip(cx_, cy_):
        return cy_ * NX + cx_

    pltpu.make_async_copy(routes_in, routes, load_sem.at[3]).start()
    pltpu.make_async_copy(gates_in, gates, load_sem.at[4]).start()
    for group in range(NX):
        for part in range(NX):
            at = (part * NX + group) * LANE
            pltpu.make_async_copy(
                cot.at[:, at : at + LANE], cx.at[group, :, part * LANE : (part + 1) * LANE], load_sem.at[0]
            ).start()
    pltpu.make_async_copy(hidden.at[0], hid, load_sem.at[1]).start()
    pltpu.make_async_copy(basis, bas, load_sem.at[2]).start()

    barrier = pltpu.get_barrier_semaphore()

    def greet(to, core):
        pl.semaphore_signal(barrier, inc=1, device_id=(to, core), device_id_type=MESH)

    def greet_z(d, carry):
        greet(dp, lax.rem(z + d, NZ) * 2 + k)
        return carry

    def greet_other(d, carry):
        greet(dp, lax.rem(z + d * ahead + NZ, NZ) * 2 + 1 - k)
        return carry

    for o in range(1, NX):
        greet(chip(lax.rem(x + o, NX), y), ex)
        greet(chip(x, lax.rem(y + o, NX)), ex)
        greet(chip(x, lax.rem(y + o, NX)), sibling)
        for near in (1, NZ - 1):
            for core in range(2):
                greet(chip(x, lax.rem(y + o, NX)), lax.rem(z + near, NZ) * 2 + core)
    greet(dp, sibling)
    lax.fori_loop(1, NZ, greet_z, 0)
    lax.fori_loop(1, HALF + 1, greet_other, 0)

    landed(routes, load_sem.at[3])
    landed(gates, load_sem.at[4])
    row = lax.broadcasted_iota(jnp.int32, (NX * NZ, TOK), 0)
    expert = lax.rem(row + (z + NZ - HALF + 1), NZ) * NX + row // NZ
    hit = jnp.zeros((NX * NZ, TOK), jnp.float32)
    gate = jnp.zeros((NX * NZ, TOK), jnp.float32)
    for n in range(routes.shape[0]):
        named = expert == routes[n : n + 1, :]
        hit = jnp.where(named, 1.0, hit)
        gate = jnp.where(named, gates[n : n + 1, :], gate)
    earlier = lax.broadcasted_iota(jnp.int32, (TOK, TOK), 0) < lax.broadcasted_iota(jnp.int32, (TOK, TOK), 1)
    before = jnp.dot(
        hit.astype(jnp.bfloat16), jnp.where(earlier, 1.0, 0.0).astype(jnp.bfloat16), preferred_element_type=jnp.float32
    )
    place = jnp.where(hit > 0.0, before + (CAP * k).astype(jnp.float32), -1.0)
    for q in range(NX):
        aux[q, 0] = place[q * NZ : (q + 1) * NZ]
        aux[q, 1] = gate[q * NZ : (q + 1) * NZ]

    landed(hid, load_sem.at[1])
    landed(bas, load_sem.at[2])
    for j in range(2):
        rows = jnp.dot(hid[j], bas[j], preferred_element_type=jnp.float32).reshape(NZ, PAIR, R)
        pz[:, j] = jnp.concatenate([rows[:, :, :LANE], rows[:, :, LANE:]], axis=1).astype(jnp.bfloat16)
    landed(cx, load_sem.at[0])

    pl.semaphore_wait(barrier, 7 * (NX - 1) + 1 + NZ - 1 + HALF)

    for o in range(1, NX):
        tx, ty = lax.rem(x + o, NX), lax.rem(y + o, NX)
        push(aux.at[ty], arx.at[x, y, k], a_send.at[o], a_recv.at[x, y], (chip(x, ty), ex))
        push(cx.at[tx], crx.at[x, y, k], c_send.at[o], c_recv.at[x, y], (chip(tx, y), ex))
    pltpu.make_async_copy(aux.at[y], arx.at[x, y, k], a_recv.at[x, y]).start()
    pltpu.make_async_copy(cx.at[x], crx.at[x, y, k], c_recv.at[x, y]).start()

    mine = pl.ds(k * 2, 2)

    def reach(d):
        i = HALF - d
        down, up = lax.rem(z - d + NZ, NZ), lax.rem(z + d, NZ)
        push(pz.at[down], prx.at[i, mine], z_send.at[i, 0], prx_sem.at[i, k], (dp, down * 2))
        if d < HALF:
            push(pz.at[up], prx.at[i, mine], z_send.at[i, 1], prx_sem.at[i, k], (dp, up * 2 + 1))

    def reached(d):
        landed(pz.at[0], z_send.at[HALF - d, 0])
        if d < HALF:
            landed(pz.at[0], z_send.at[HALF - d, 1])

    for d in range(HALF, 0, -1):
        reach(d)

    @pl.when(k == 0)
    def _():
        push(pz.at[z], prx.at[0, mine], z_send.at[0, 1], prx_sem.at[0, k], (dp, sibling))

    @pl.when(k == 1)
    def _():
        pltpu.make_async_copy(pz.at[z], prx.at[0, mine], prx_sem.at[0, k]).start()

    def share_slots(sx, sy):
        push(arx.at[sx, sy, k], arx.at[sx, sy, k], sa_send.at[sx, sy], sa_recv.at[sx, sy], (dp, sibling))

    def share_columns(sx, sy):
        push(crx.at[sx, sy, k], crx.at[sx, sy, k], sc_send.at[sx, sy], sc_recv.at[sx, sy], (dp, sibling))

    def forward(o):
        sy = lax.rem(y - o + NX, NX)
        landed(arx.at[x, sy, k], a_recv.at[x, sy])
        for t in range(1, NX):
            push(arx.at[x, sy, k], arx.at[x, sy, k], ax_send.at[o, t], a_recv.at[x, sy], (chip(lax.rem(x + t, NX), y), ex))
        share_slots(x, sy)
        sx = lax.rem(x - o + NX, NX)
        landed(crx.at[sx, y, k], c_recv.at[sx, y])
        for t in range(1, NX):
            push(crx.at[sx, y, k], crx.at[sx, y, k], cy_send.at[o, t], c_recv.at[sx, y], (chip(x, lax.rem(y + t, NX)), ex))
        share_columns(sx, y)

    def spread_y(i):
        for core in range(2):
            landed(prx.at[i, pl.ds(core * 2, 2)], prx_sem.at[i, core])
        for t in range(1, NX):
            ty = lax.rem(y + t, NX)
            push(prx.at[i, ty], pg.at[i, x, y], p1_send.at[i, t], p1_recv.at[i, y], (chip(x, ty), ex))
        pltpu.make_async_copy(prx.at[i, y], pg.at[i, x, y], p1_recv.at[i, y]).start()

    def spread_x(i):
        for sy in range(NX):
            landed(pg.at[i, x, sy], p1_recv.at[i, sy])
        for t in range(1, NX):
            push(pg.at[i, x], pg.at[i, x], p2_send.at[i, t], p2_recv.at[i, x], (chip(lax.rem(x + t, NX), y), ex))

    def receive(o, t):
        sx, sy = lax.rem(x - t + NX, NX), lax.rem(y - o + NX, NX)
        landed(arx.at[sx, sy, k], a_recv.at[sx, sy])
        share_slots(sx, sy)
        sx, sy = lax.rem(x - o + NX, NX), lax.rem(y - t + NX, NX)
        landed(crx.at[sx, sy, k], c_recv.at[sx, sy])
        share_columns(sx, sy)

    first = pl.multiple_of((1 - k) * HALF, HALF)
    slot = lax.broadcasted_iota(jnp.int32, (HALF, PAIR, 2 * TOK), 1).astype(jnp.float32)

    def rows_of(sx, sy):
        landed(arx.at[sx, sy, 1 - k], sa_recv.at[sx, sy])
        landed(crx.at[sx, sy, 1 - k], sc_recv.at[sx, sy])
        place = jnp.concatenate([arx[sx, sy, c, 0, pl.ds(first, HALF), :] for c in range(2)], axis=1)
        gate = jnp.concatenate([arx[sx, sy, c, 1, pl.ds(first, HALF), :] for c in range(2)], axis=1)
        here = slot == place[:, None, :]
        weight = jnp.sum(jnp.where(here, gate[:, None, :], 0.0), axis=2, keepdims=True)
        pick = jnp.where(here, 1.0, 0.0).reshape(HALF * PAIR, 2 * TOK).astype(jnp.bfloat16)
        rows = jnp.dot(pick, crx[sx, sy].reshape(2 * TOK, WIDE), preferred_element_type=jnp.float32)
        return rows.reshape(HALF, PAIR, WIDE) * weight

    def build(pair, carry):
        sx, sy = pair // 2, 2 * lax.rem(pair, 2)
        both = jnp.concatenate([rows_of(sx, sy), rows_of(sx, sy + 1)], axis=1)
        tab[:, pair] = both.astype(jnp.bfloat16)
        return carry

    todo = [(o, t) for o in range(NX) for t in range(1, NX)]

    def take(n):
        for _ in range(n):
            receive(*todo.pop(0))

    def more(d):
        reached(d + 3)
        reach(d)

    onward = lax.rem(z + ahead + NZ, NZ) * 2 + k

    def turn(i):
        for t in range(1, NX):
            sx = lax.rem(x + t, NX)
            landed(pg.at[i, sx], p2_recv.at[i, sx])
        got = pg[i].astype(jnp.float32).reshape(PLANE, 2, PAIR, LANE)
        for h in range(2):
            pt[i, h * LANE : (h + 1) * LANE, :] = got[:, h].reshape(PLANE * PAIR, LANE).T.astype(jnp.bfloat16)

    def block(i, b):
        table = tab[jnp.where(k == 0, HALF - 1 - i, (i + HALF - 1) % HALF), :, :, b * LANE : (b + 1) * LANE]
        return jnp.dot(pt[i], table.reshape(PLANE * PAIR, LANE), preferred_element_type=jnp.float32)

    def arrived(i, b):
        landed(rxs.at[i, b], s_recv.at[i, b])
        landed(rxq.at[i, b], q_recv.at[i, b])
        return rxq[i, b].astype(jnp.int32).astype(jnp.float32) * rxs[i, b, 0:1, :]

    def code(value, i, b):
        most = jnp.maximum(jnp.max(jnp.abs(value), axis=0, keepdims=True), 1e-33)
        txq[i, b] = jnp.round(value * (FULL / most)).astype(jnp.int32).astype(jnp.int16)
        txs[i, b] = jnp.broadcast_to(most * (1.0 / FULL), (8, LANE))

    def push_on(i, b):
        push(txs.at[i, b], rxs.at[i + 1, b], s_send.at[i, b], s_recv.at[i + 1, b], (dp, onward))
        push(txq.at[i, b], rxq.at[i + 1, b], q_send.at[i, b], q_recv.at[i + 1, b], (dp, onward))

    owner_core = y // 2
    part = lax.rem(y, 2)

    def here(b):
        return (y == b) & (owner_core == k)

    def push_owner(i, b, source, plane):
        owner = (b * NX + x, plane * 2 + owner_core)
        push(txs.at[i, b], fins.at[source, part], s_send.at[i, b], fs_recv.at[source, part], owner)
        push(txq.at[i, b], finq.at[source, part], q_send.at[i, b], fq_recv.at[source, part], owner)

    def hop(i):
        turn(i)
        for b in range(NX):
            value = block(i, b)
            if i == 0:
                code(value, 0, b)

                @pl.when(k == 0)
                def _():
                    push_on(0, b)

                @pl.when((k == 1) & here(b))
                def _():
                    pltpu.make_async_copy(txs.at[0, b], fins.at[2, part], fs_recv.at[2, part]).start()
                    pltpu.make_async_copy(txq.at[0, b], finq.at[2, part], fq_recv.at[2, part]).start()

                @pl.when((k == 1) & jnp.logical_not(here(b)))
                def _():
                    push_owner(0, b, 2, z)

            elif i == 1:
                own[...] = value

                @pl.when(k == 0)
                def _():
                    own[...] += arrived(1, b)

                code(own[...], 1, b)
                push_on(1, b)
            else:
                code(value + arrived(i, b), i, b)
                if i < HALF - 1:
                    push_on(i, b)
                else:
                    push_owner(i, b, k, lax.rem(z + ahead + NZ, NZ))

    for o in range(NX):
        forward(o)
    for i in range(HALF):
        spread_y(i)
        if i > 2:
            spread_x(i - 3)
        if i % 2:
            take(3)
    lax.fori_loop(0, 4, build, 0)
    spread_x(5)
    lax.fori_loop(4, 6, build, 0)
    spread_x(6)
    lax.fori_loop(6, 8, build, 0)
    spread_x(7)
    for i in range(HALF):
        hop(i)

    for j in range(2):
        total = None
        for core in (2, 0, 1):
            landed(fins.at[core, j], fs_recv.at[core, j])
            landed(finq.at[core, j], fq_recv.at[core, j])
            value = finq[core, j].astype(jnp.int32).astype(jnp.float32) * fins[core, j, 0:1, :]
            total = value if total is None else total + value
        out[j] = total

    for d in range(HALF, 0, -1):
        reached(d)

    @pl.when(k == 0)
    def _():
        landed(pz.at[0], z_send.at[0, 1])

    def left(i, carry):
        for t in range(1, NX):
            landed(pz.at[0, 0], p1_send.at[i, t])
            landed(pg.at[i, 0], p2_send.at[i, t])
        return carry

    lax.fori_loop(0, HALF, left, 0)

    def gone(o, carry):
        for t in range(NX):
            landed(aux.at[0], sa_send.at[o, t])
            landed(cx.at[0], sc_send.at[o, t])
        for t in range(1, NX):
            landed(aux.at[0], ax_send.at[o, t])
            landed(cx.at[0], cy_send.at[o, t])

        @pl.when(o > 0)
        def _():
            landed(aux.at[0], a_send.at[o])
            landed(cx.at[0], c_send.at[o])

        return carry

    lax.fori_loop(0, NX, gone, 0)

    def sent(i, carry):
        for b in range(NX):
            landed(txs.at[i, b], s_send.at[i, b])
            landed(txq.at[i, b], q_send.at[i, b])
        return carry

    lax.fori_loop(1, HALF, sent, 0)

    for b in range(NX):

        @pl.when((k == 0) | jnp.logical_not(here(b)))
        def _():
            landed(txs.at[0, b], s_send.at[0, b])
            landed(txq.at[0, b], q_send.at[0, b])


def exchange(cotangent, routes, gates, hidden, basis):
    dma = pltpu.SemaphoreType.DMA
    square = dma((NX, NX))
    return pl.pallas_call(
        kernel,
        out_shape=jax.ShapeDtypeStruct((2, R, LANE), jnp.float32),
        in_specs=[pl.BlockSpec(memory_space=pltpu.HBM)] * 5,
        out_specs=pl.BlockSpec(memory_space=pltpu.VMEM),
        scratch_shapes=[
            pltpu.VMEM(routes.shape, jnp.int32),
            pltpu.VMEM(gates.shape, jnp.float32),
            pltpu.VMEM((NX, TOK, WIDE), jnp.bfloat16),
            pltpu.VMEM((NX, 2, NZ, TOK), jnp.float32),
            pltpu.VMEM(hidden.shape[1:], jnp.bfloat16),
            pltpu.VMEM(basis.shape, jnp.bfloat16),
            pltpu.VMEM((NZ, 2, 2 * PAIR, LANE), jnp.bfloat16),
            dma((5,)),
            pltpu.VMEM((HALF, NX, 2 * PAIR, LANE), jnp.bfloat16),
            pltpu.VMEM((HALF, NX, NX, 2 * PAIR, LANE), jnp.bfloat16),
            pltpu.VMEM((NX, NX, 2, TOK, WIDE), jnp.bfloat16),
            pltpu.VMEM((NX, NX, 2, 2, NZ, TOK), jnp.float32),
            pltpu.VMEM((HALF, PLANE // 2, 2 * PAIR, WIDE), jnp.bfloat16),
            pltpu.VMEM((HALF, R, PLANE * PAIR), jnp.bfloat16),
            pltpu.VMEM((R, LANE), jnp.float32),
            pltpu.VMEM((HALF + 1, NX, R, LANE), jnp.int16),
            pltpu.VMEM((HALF + 1, NX, 8, LANE), jnp.float32),
            pltpu.VMEM((HALF + 1, NX, R, LANE), jnp.int16),
            pltpu.VMEM((HALF + 1, NX, 8, LANE), jnp.float32),
            pltpu.VMEM((3, 2, R, LANE), jnp.int16),
            pltpu.VMEM((3, 2, 8, LANE), jnp.float32),
            dma((HALF, 2)),
            dma((HALF, 2)),
            dma((NX,)), dma((NX,)), square, square, square, square,
            square, square, square, square,
            dma((HALF, NX)), dma((HALF, NX)), dma((HALF, NX)), dma((HALF, NX)),
            dma((HALF, NX)), dma((HALF, NX)),
            dma((HALF + 1, NX)), dma((HALF + 1, NX)),
            dma((3, 2)), dma((3, 2)),
        ],
        compiler_params=pltpu.CompilerParams(
            collective_id=0, has_side_effects=True, vmem_limit_bytes=56 * 1024 * 1024
        ),
        cost_estimate=pl.CostEstimate(flops=2_700_000_000, bytes_accessed=4_000_000, transcendentals=0),
    )(cotangent, routes, gates, hidden, basis)


def body(cotangent, routes, gate_weights, hidden, galore_basis, moment, second):
    gradient = exchange(cotangent, routes.T, gate_weights.T, hidden, galore_basis)
    new_moment = beta_one * moment + (1.0 - beta_one) * gradient
    new_second = beta_two * second + (1.0 - beta_two) * gradient * gradient
    update = (
        new_moment
        / (1.0 - beta_one**STEP)
        / (jnp.sqrt(new_second / (1.0 - beta_two**STEP)) + epsilon)
    )
    return (new_moment, new_second, update)


def solution(mesh):
    placed = (
        P(("dp", "expert"), None),
        P(("dp", "expert"), None),
        P(("dp", "expert"), None),
        P("dp", "expert", None, None),
        P("expert", None, None),
        P("expert", None, "dp"),
        P("expert", None, "dp"),
    )
    return jax.shard_map(
        body,
        mesh=mesh,
        in_specs=placed,
        out_specs=(P("expert", None, "dp"), P("expert", None, "dp"), P("expert", None, "dp")),
        check_vma=False,
    )
```

```python
import functools

import jax
import jax.numpy as jnp
from jax import lax
from jax.experimental import pallas as pl
from jax.experimental.pallas import tpu as pltpu
from jax.sharding import PartitionSpec as P

STEP = 100
MESH = pl.DeviceIdType.MESH

beta_one = 0.9
beta_two = 0.999
epsilon = 1e-08

NX = 4
NZ = 16
PLANE = NX * NX
HALF = 8
CAP = 20
PAIR = 2 * CAP
R = 256
LANE = 128
TOK = 128
WIDE = NX * LANE
FULL = 32767.0


def landed(ref, sem):
    pltpu.make_async_copy(ref, ref, sem).wait()


def kernel(
    cot, routes_in, gates_in, hidden, basis, out,
    routes, gates, cx, aux, hid, bas, pz, load_sem, prx, pg, crx, arx, tab, pt, own, rxq, rxs, txq, txs, finq, fins,
    z_send, prx_sem, c_send, a_send, c_recv, a_recv, cy_send, ax_send,
    sc_send, sa_send, sc_recv, sa_recv, p1_send, p1_recv, p2_send, p2_recv,
    q_send, s_send, q_recv, s_recv, fq_recv, fs_recv,
):
    dp = lax.axis_index("dp")
    ex = lax.axis_index("expert")
    x, y = lax.rem(dp, NX), dp // NX
    z, k = ex // 2, lax.rem(ex, 2)
    sibling = z * 2 + 1 - k
    ahead = 1 - 2 * k

    def push(src, dst, send, recv, device):
        pltpu.make_async_remote_copy(
            src_ref=src, dst_ref=dst, send_sem=send, recv_sem=recv, device_id=device, device_id_type=MESH
        ).start()

    def chip(cx_, cy_):
        return cy_ * NX + cx_

    barrier = pltpu.get_barrier_semaphore()

    def greet(to, core):
        pl.semaphore_signal(barrier, inc=1, device_id=(to, core), device_id_type=MESH)

    def greet_z(d, carry):
        greet(dp, lax.rem(z + d, NZ) * 2 + k)
        return carry

    def greet_other(d, carry):
        greet(dp, lax.rem(z + d * ahead + NZ, NZ) * 2 + 1 - k)
        return carry

    lax.fori_loop(1, NZ, greet_z, 0)
    lax.fori_loop(1, HALF + 1, greet_other, 0)
    for o in range(1, NX):
        greet(chip(lax.rem(x + o, NX), y), ex)
        greet(chip(x, lax.rem(y + o, NX)), ex)
        greet(chip(x, lax.rem(y + o, NX)), sibling)
        for near in (1, NZ - 1):
            for core in range(2):
                greet(chip(x, lax.rem(y + o, NX)), lax.rem(z + near, NZ) * 2 + core)
    greet(dp, sibling)

    pltpu.make_async_copy(routes_in, routes, load_sem.at[3]).start()
    pltpu.make_async_copy(gates_in, gates, load_sem.at[4]).start()
    for group in range(NX):
        for part in range(NX):
            at = (part * NX + group) * LANE
            pltpu.make_async_copy(
                cot.at[:, at : at + LANE], cx.at[group, :, part * LANE : (part + 1) * LANE], load_sem.at[0]
            ).start()
    pltpu.make_async_copy(hidden.at[0], hid, load_sem.at[1]).start()
    pltpu.make_async_copy(basis, bas, load_sem.at[2]).start()

    landed(routes, load_sem.at[3])
    landed(gates, load_sem.at[4])
    row = lax.broadcasted_iota(jnp.int32, (NX * NZ, TOK), 0)
    expert = lax.rem(row + (z + NZ - HALF + 1), NZ) * NX + row // NZ
    hit = jnp.zeros((NX * NZ, TOK), jnp.float32)
    gate = jnp.zeros((NX * NZ, TOK), jnp.float32)
    for n in range(routes.shape[0]):
        named = expert == routes[n : n + 1, :]
        hit = jnp.where(named, 1.0, hit)
        gate = jnp.where(named, gates[n : n + 1, :], gate)
    earlier = lax.broadcasted_iota(jnp.int32, (TOK, TOK), 0) < lax.broadcasted_iota(jnp.int32, (TOK, TOK), 1)
    before = jnp.dot(
        hit.astype(jnp.bfloat16), jnp.where(earlier, 1.0, 0.0).astype(jnp.bfloat16), preferred_element_type=jnp.float32
    )
    place = jnp.where(hit > 0.0, before + (CAP * k).astype(jnp.float32), -1.0)
    for q in range(NX):
        aux[q, 0] = place[q * NZ : (q + 1) * NZ]
        aux[q, 1] = gate[q * NZ : (q + 1) * NZ]

    landed(hid, load_sem.at[1])
    landed(bas, load_sem.at[2])
    for j in range(2):
        rows = jnp.dot(hid[j], bas[j], preferred_element_type=jnp.float32).reshape(NZ, PAIR, R)
        pz[:, j] = jnp.concatenate([rows[:, :, :LANE], rows[:, :, LANE:]], axis=1).astype(jnp.bfloat16)
    landed(cx, load_sem.at[0])

    pl.semaphore_wait(barrier, 7 * (NX - 1) + 1 + NZ - 1 + HALF)

    for o in range(1, NX):
        tx, ty = lax.rem(x + o, NX), lax.rem(y + o, NX)
        push(aux.at[ty], arx.at[x, y, k], a_send.at[o], a_recv.at[x, y], (chip(x, ty), ex))
        push(cx.at[tx], crx.at[x, y, k], c_send.at[o], c_recv.at[x, y], (chip(tx, y), ex))
    pltpu.make_async_copy(aux.at[y], arx.at[x, y, k], a_recv.at[x, y]).start()
    pltpu.make_async_copy(cx.at[x], crx.at[x, y, k], c_recv.at[x, y]).start()

    mine = pl.ds(k * 2, 2)

    def reach(d):
        i = HALF - d
        down, up = lax.rem(z - d + NZ, NZ), lax.rem(z + d, NZ)
        push(pz.at[down], prx.at[i, mine], z_send.at[i, 0], prx_sem.at[i, k], (dp, down * 2))
        if d < HALF:
            push(pz.at[up], prx.at[i, mine], z_send.at[i, 1], prx_sem.at[i, k], (dp, up * 2 + 1))

    def reached(d):
        landed(pz.at[0], z_send.at[HALF - d, 0])
        if d < HALF:
            landed(pz.at[0], z_send.at[HALF - d, 1])

    for d in range(HALF, 0, -1):
        reach(d)

    @pl.when(k == 0)
    def _():
        push(pz.at[z], prx.at[0, mine], z_send.at[0, 1], prx_sem.at[0, k], (dp, sibling))

    @pl.when(k == 1)
    def _():
        pltpu.make_async_copy(pz.at[z], prx.at[0, mine], prx_sem.at[0, k]).start()

    def share_slots(sx, sy):
        push(arx.at[sx, sy, k], arx.at[sx, sy, k], sa_send.at[sx, sy], sa_recv.at[sx, sy], (dp, sibling))

    def share_columns(sx, sy):
        push(crx.at[sx, sy, k], crx.at[sx, sy, k], sc_send.at[sx, sy], sc_recv.at[sx, sy], (dp, sibling))

    def forward(o):
        sy = lax.rem(y - o + NX, NX)
        landed(arx.at[x, sy, k], a_recv.at[x, sy])
        for t in range(1, NX):
            push(arx.at[x, sy, k], arx.at[x, sy, k], ax_send.at[o, t], a_recv.at[x, sy], (chip(lax.rem(x + t, NX), y), ex))
        share_slots(x, sy)
        sx = lax.rem(x - o + NX, NX)
        landed(crx.at[sx, y, k], c_recv.at[sx, y])
        for t in (1, NX - 1):
            push(crx.at[sx, y, k], crx.at[sx, y, k], cy_send.at[o, t], c_recv.at[sx, y], (chip(x, lax.rem(y + t, NX)), ex))
        share_columns(sx, y)

    def spread_y(i):
        for core in range(2):
            landed(prx.at[i, pl.ds(core * 2, 2)], prx_sem.at[i, core])
        for t in range(1, NX):
            ty = lax.rem(y + t, NX)
            push(prx.at[i, ty], pg.at[i, x, y], p1_send.at[i, t], p1_recv.at[i, y], (chip(x, ty), ex))
        pltpu.make_async_copy(prx.at[i, y], pg.at[i, x, y], p1_recv.at[i, y]).start()

    def spread_x(i):
        for sy in range(NX):
            landed(pg.at[i, x, sy], p1_recv.at[i, sy])
        for t in range(1, NX):
            push(pg.at[i, x], pg.at[i, x], p2_send.at[i, t], p2_recv.at[i, x], (chip(lax.rem(x + t, NX), y), ex))

    def receive(o, t):
        sx, sy = lax.rem(x - t + NX, NX), lax.rem(y - o + NX, NX)
        landed(arx.at[sx, sy, k], a_recv.at[sx, sy])
        share_slots(sx, sy)
        sx, sy = lax.rem(x - o + NX, NX), lax.rem(y - t + NX, NX)
        landed(crx.at[sx, sy, k], c_recv.at[sx, sy])
        if t == (1 if o % 2 == 0 else NX - 1):
            over = chip(x, lax.rem(y + t, NX))
            push(crx.at[sx, sy, k], crx.at[sx, sy, k], cy_send.at[o, 2], c_recv.at[sx, sy], (over, ex))
        share_columns(sx, sy)

    first = pl.multiple_of((1 - k) * HALF, HALF)
    slot = lax.broadcasted_iota(jnp.int32, (HALF, PAIR, 2 * TOK), 1).astype(jnp.float32)

    def rows_of(sx, sy):
        landed(arx.at[sx, sy, 1 - k], sa_recv.at[sx, sy])
        landed(crx.at[sx, sy, 1 - k], sc_recv.at[sx, sy])
        place = jnp.concatenate([arx[sx, sy, c, 0, pl.ds(first, HALF), :] for c in range(2)], axis=1)
        gate = jnp.concatenate([arx[sx, sy, c, 1, pl.ds(first, HALF), :] for c in range(2)], axis=1)
        here = slot == place[:, None, :]
        weight = jnp.sum(jnp.where(here, gate[:, None, :], 0.0), axis=2, keepdims=True)
        pick = jnp.where(here, 1.0, 0.0).reshape(HALF * PAIR, 2 * TOK).astype(jnp.bfloat16)
        rows = jnp.dot(pick, crx[sx, sy].reshape(2 * TOK, WIDE), preferred_element_type=jnp.float32)
        return rows.reshape(HALF, PAIR, WIDE) * weight

    def build(pair, carry):
        sx, sy = pair // 2, 2 * lax.rem(pair, 2)
        both = jnp.concatenate([rows_of(sx, sy), rows_of(sx, sy + 1)], axis=1)
        tab[:, pair] = both.astype(jnp.bfloat16)
        return carry

    todo = [(0, 1), (0, 3)]
    for o in range(1, NX):
        todo += [(o, 1), (o, 3), (o - 1, 2)]
    todo.append((NX - 1, 2))

    def take(n):
        for _ in range(n):
            receive(*todo.pop(0))

    def more(d):
        reached(d + 3)
        reach(d)

    onward = lax.rem(z + ahead + NZ, NZ) * 2 + k

    def turn(i):
        for t in range(1, NX):
            sx = lax.rem(x + t, NX)
            landed(pg.at[i, sx], p2_recv.at[i, sx])
        got = pg[i].astype(jnp.float32).reshape(PLANE, 2, PAIR, LANE)
        for h in range(2):
            pt[i, h * LANE : (h + 1) * LANE, :] = got[:, h].reshape(PLANE * PAIR, LANE).T.astype(jnp.bfloat16)

    def block(i, b):
        table = tab[jnp.where(k == 0, HALF - 1 - i, (i + HALF - 1) % HALF), :, :, b * LANE : (b + 1) * LANE]
        return jnp.dot(pt[i], table.reshape(PLANE * PAIR, LANE), preferred_element_type=jnp.float32)

    def arrived(i, b):
        landed(rxs.at[i, b], s_recv.at[i, b])
        landed(rxq.at[i, b], q_recv.at[i, b])
        return rxq[i, b].astype(jnp.int32).astype(jnp.float32) * rxs[i, b, 0:1, :]

    def code(value, i, b):
        most = jnp.maximum(jnp.max(jnp.abs(value), axis=0, keepdims=True), 1e-33)
        txq[i, b] = jnp.round(value * (FULL / most)).astype(jnp.int32).astype(jnp.int16)
        txs[i, b] = jnp.broadcast_to(most * (1.0 / FULL), (8, LANE))

    def push_on(i, b):
        push(txs.at[i, b], rxs.at[i + 1, b], s_send.at[i, b], s_recv.at[i + 1, b], (dp, onward))
        push(txq.at[i, b], rxq.at[i + 1, b], q_send.at[i, b], q_recv.at[i + 1, b], (dp, onward))

    owner_core = y // 2
    part = lax.rem(y, 2)

    def here(b):
        return (y == b) & (owner_core == k)

    def push_owner(i, b, source, plane):
        owner = (b * NX + x, plane * 2 + owner_core)
        push(txs.at[i, b], fins.at[source, part], s_send.at[i, b], fs_recv.at[source, part], owner)
        push(txq.at[i, b], finq.at[source, part], q_send.at[i, b], fq_recv.at[source, part], owner)

    def hop(i):
        turn(i)
        for b in range(NX):
            own[b] = block(i, b)
        for b in range(NX):
            value = own[b]
            if i == 0:
                code(value, 0, b)

                @pl.when(k == 0)
                def _():
                    push_on(0, b)

                @pl.when((k == 1) & here(b))
                def _():
                    pltpu.make_async_copy(txs.at[0, b], fins.at[2, part], fs_recv.at[2, part]).start()
                    pltpu.make_async_copy(txq.at[0, b], finq.at[2, part], fq_recv.at[2, part]).start()

                @pl.when((k == 1) & jnp.logical_not(here(b)))
                def _():
                    push_owner(0, b, 2, z)

            elif i == 1:
                @pl.when(k == 0)
                def _():
                    own[b] += arrived(1, b)

                code(own[b], 1, b)
                push_on(1, b)
            else:
                code(value + arrived(i, b), i, b)
                if i < HALF - 1:
                    push_on(i, b)
                else:
                    push_owner(i, b, k, lax.rem(z + ahead + NZ, NZ))

    forward(0)
    forward(1)
    forward(2)
    forward(3)
    take(2)
    spread_y(0)
    take(3)
    spread_y(1)
    take(3)
    spread_x(0)
    spread_x(1)
    take(3)
    spread_y(2)
    spread_y(3)
    spread_y(4)
    take(1)
    spread_x(2)
    spread_y(5)
    spread_x(3)
    spread_y(6)
    spread_x(4)
    spread_y(7)
    lax.fori_loop(0, 4, build, 0)
    spread_x(5)
    lax.fori_loop(4, 8, build, 0)
    hop(0)
    spread_x(6)
    hop(1)
    spread_x(7)
    hop(2)
    hop(3)
    hop(4)
    hop(5)
    hop(6)
    hop(7)

    for j in range(2):
        total = None
        for core in (2, 0, 1):
            landed(fins.at[core, j], fs_recv.at[core, j])
            landed(finq.at[core, j], fq_recv.at[core, j])
            value = finq[core, j].astype(jnp.int32).astype(jnp.float32) * fins[core, j, 0:1, :]
            total = value if total is None else total + value
        out[j] = total

    for d in range(HALF, 0, -1):
        reached(d)

    @pl.when(k == 0)
    def _():
        landed(pz.at[0], z_send.at[0, 1])

    def left(i, carry):
        for t in range(1, NX):
            landed(pz.at[0, 0], p1_send.at[i, t])
            landed(pg.at[i, 0], p2_send.at[i, t])
        return carry

    lax.fori_loop(0, HALF, left, 0)

    def gone(o, carry):
        for t in range(NX):
            landed(aux.at[0], sa_send.at[o, t])
            landed(cx.at[0], sc_send.at[o, t])
        for t in range(1, NX):
            landed(aux.at[0], ax_send.at[o, t])
            landed(cx.at[0], cy_send.at[o, t])

        @pl.when(o > 0)
        def _():
            landed(aux.at[0], a_send.at[o])
            landed(cx.at[0], c_send.at[o])

        return carry

    lax.fori_loop(0, NX, gone, 0)

    def sent(i, carry):
        for b in range(NX):
            landed(txs.at[i, b], s_send.at[i, b])
            landed(txq.at[i, b], q_send.at[i, b])
        return carry

    lax.fori_loop(1, HALF, sent, 0)

    for b in range(NX):

        @pl.when((k == 0) | jnp.logical_not(here(b)))
        def _():
            landed(txs.at[0, b], s_send.at[0, b])
            landed(txq.at[0, b], q_send.at[0, b])


def exchange(cotangent, routes, gates, hidden, basis):
    dma = pltpu.SemaphoreType.DMA
    square = dma((NX, NX))
    return pl.pallas_call(
        kernel,
        out_shape=jax.ShapeDtypeStruct((2, R, LANE), jnp.float32),
        in_specs=[pl.BlockSpec(memory_space=pltpu.HBM)] * 5,
        out_specs=pl.BlockSpec(memory_space=pltpu.VMEM),
        scratch_shapes=[
            pltpu.VMEM(routes.shape, jnp.int32),
            pltpu.VMEM(gates.shape, jnp.float32),
            pltpu.VMEM((NX, TOK, WIDE), jnp.bfloat16),
            pltpu.VMEM((NX, 2, NZ, TOK), jnp.float32),
            pltpu.VMEM(hidden.shape[1:], jnp.bfloat16),
            pltpu.VMEM(basis.shape, jnp.bfloat16),
            pltpu.VMEM((NZ, 2, 2 * PAIR, LANE), jnp.bfloat16),
            dma((5,)),
            pltpu.VMEM((HALF, NX, 2 * PAIR, LANE), jnp.bfloat16),
            pltpu.VMEM((HALF, NX, NX, 2 * PAIR, LANE), jnp.bfloat16),
            pltpu.VMEM((NX, NX, 2, TOK, WIDE), jnp.bfloat16),
            pltpu.VMEM((NX, NX, 2, 2, NZ, TOK), jnp.float32),
            pltpu.VMEM((HALF, PLANE // 2, 2 * PAIR, WIDE), jnp.bfloat16),
            pltpu.VMEM((HALF, R, PLANE * PAIR), jnp.bfloat16),
            pltpu.VMEM((NX, R, LANE), jnp.float32),
            pltpu.VMEM((HALF + 1, NX, R, LANE), jnp.int16),
            pltpu.VMEM((HALF + 1, NX, 8, LANE), jnp.float32),
            pltpu.VMEM((HALF + 1, NX, R, LANE), jnp.int16),
            pltpu.VMEM((HALF + 1, NX, 8, LANE), jnp.float32),
            pltpu.VMEM((3, 2, R, LANE), jnp.int16),
            pltpu.VMEM((3, 2, 8, LANE), jnp.float32),
            dma((HALF, 2)),
            dma((HALF, 2)),
            dma((NX,)), dma((NX,)), square, square, square, square,
            square, square, square, square,
            dma((HALF, NX)), dma((HALF, NX)), dma((HALF, NX)), dma((HALF, NX)),
            dma((HALF, NX)), dma((HALF, NX)),
            dma((HALF + 1, NX)), dma((HALF + 1, NX)),
            dma((3, 2)), dma((3, 2)),
        ],
        compiler_params=pltpu.CompilerParams(
            collective_id=0, has_side_effects=True, vmem_limit_bytes=56 * 1024 * 1024
        ),
        cost_estimate=pl.CostEstimate(flops=2_700_000_000, bytes_accessed=4_000_000, transcendentals=0),
    )(cotangent, routes, gates, hidden, basis)


def body(cotangent, routes, gate_weights, hidden, galore_basis, moment, second):
    gradient = exchange(cotangent, routes.T, gate_weights.T, hidden, galore_basis)
    new_moment = beta_one * moment + (1.0 - beta_one) * gradient
    new_second = beta_two * second + (1.0 - beta_two) * gradient * gradient
    update = (
        new_moment
        / (1.0 - beta_one**STEP)
        / (jnp.sqrt(new_second / (1.0 - beta_two**STEP)) + epsilon)
    )
    return (new_moment, new_second, update)


def solution(mesh):
    placed = (
        P(("dp", "expert"), None),
        P(("dp", "expert"), None),
        P(("dp", "expert"), None),
        P("dp", "expert", None, None),
        P("expert", None, None),
        P("expert", None, "dp"),
        P("expert", None, "dp"),
    )
    return jax.shard_map(
        body,
        mesh=mesh,
        in_specs=placed,
        out_specs=(P("expert", None, "dp"), P("expert", None, "dp"), P("expert", None, "dp")),
        check_vma=False,
    )
```

```python
import functools

import jax
import jax.numpy as jnp
from jax import lax
from jax.experimental import pallas as pl
from jax.experimental.pallas import tpu as pltpu
from jax.sharding import PartitionSpec as P

STEP = 100
MESH = pl.DeviceIdType.MESH

beta_one = 0.9
beta_two = 0.999
epsilon = 1e-08

NX = 4
NZ = 16
PLANE = NX * NX
HALF = 8
CAP = 20
PAIR = 2 * CAP
R = 256
LANE = 128
TOK = 128
WIDE = NX * LANE
FULL = 32767.0


def landed(ref, sem):
    pltpu.make_async_copy(ref, ref, sem).wait()


def kernel(
    cot, routes_in, gates_in, hidden, basis, out,
    routes, gates, cx, aux, hid, bas, pz, load_sem, prx, pg, crx, arx, tab, pt, own, rxq, rxs, txq, txs, finq, fins,
    z_send, prx_sem, c_send, a_send, c_recv, a_recv, cy_send, ax_send,
    sc_send, sa_send, sc_recv, sa_recv, p1_send, p1_recv, p2_send, p2_recv,
    q_send, s_send, q_recv, s_recv, fq_recv, fs_recv,
):
    dp = lax.axis_index("dp")
    ex = lax.axis_index("expert")
    x, y = lax.rem(dp, NX), dp // NX
    z, k = ex // 2, lax.rem(ex, 2)
    sibling = z * 2 + 1 - k
    ahead = 1 - 2 * k

    def push(src, dst, send, recv, device):
        pltpu.make_async_remote_copy(
            src_ref=src, dst_ref=dst, send_sem=send, recv_sem=recv, device_id=device, device_id_type=MESH
        ).start()

    def chip(cx_, cy_):
        return cy_ * NX + cx_

    pltpu.make_async_copy(hidden.at[0], hid, load_sem.at[1]).start()
    pltpu.make_async_copy(basis, bas, load_sem.at[2]).start()
    pltpu.make_async_copy(routes_in, routes, load_sem.at[3]).start()
    pltpu.make_async_copy(gates_in, gates, load_sem.at[4]).start()

    barrier = pltpu.get_barrier_semaphore()

    def greet(to, core):
        pl.semaphore_signal(barrier, inc=1, device_id=(to, core), device_id_type=MESH)

    def greet_z(d, carry):
        greet(dp, lax.rem(z + d, NZ) * 2 + k)
        return carry

    def greet_other(d, carry):
        greet(dp, lax.rem(z + d * ahead + NZ, NZ) * 2 + 1 - k)
        return carry

    lax.fori_loop(1, NZ, greet_z, 0)
    lax.fori_loop(1, HALF + 1, greet_other, 0)
    for o in range(1, NX):
        greet(chip(lax.rem(x + o, NX), y), ex)
        greet(chip(x, lax.rem(y + o, NX)), ex)
        greet(chip(x, lax.rem(y + o, NX)), sibling)
        for near in (1, NZ - 1):
            for core in range(2):
                greet(chip(x, lax.rem(y + o, NX)), lax.rem(z + near, NZ) * 2 + core)
    greet(dp, sibling)

    for group in range(NX):
        for part in range(NX):
            at = (part * NX + group) * LANE
            pltpu.make_async_copy(
                cot.at[:, at : at + LANE], cx.at[group, :, part * LANE : (part + 1) * LANE], load_sem.at[0]
            ).start()

    landed(routes, load_sem.at[3])
    landed(gates, load_sem.at[4])
    row = lax.broadcasted_iota(jnp.int32, (NX * NZ, TOK), 0)
    expert = lax.rem(row + (z + NZ - HALF + 1), NZ) * NX + row // NZ
    hit = jnp.zeros((NX * NZ, TOK), jnp.float32)
    gate = jnp.zeros((NX * NZ, TOK), jnp.float32)
    for n in range(routes.shape[0]):
        named = expert == routes[n : n + 1, :]
        hit = jnp.where(named, 1.0, hit)
        gate = jnp.where(named, gates[n : n + 1, :], gate)
    earlier = lax.broadcasted_iota(jnp.int32, (TOK, TOK), 0) < lax.broadcasted_iota(jnp.int32, (TOK, TOK), 1)
    before = jnp.dot(
        hit.astype(jnp.bfloat16), jnp.where(earlier, 1.0, 0.0).astype(jnp.bfloat16), preferred_element_type=jnp.float32
    )
    place = jnp.where(hit > 0.0, before + (CAP * k).astype(jnp.float32), -1.0)
    for q in range(NX):
        aux[q, 0] = place[q * NZ : (q + 1) * NZ]
        aux[q, 1] = gate[q * NZ : (q + 1) * NZ]

    landed(hid, load_sem.at[1])
    landed(bas, load_sem.at[2])
    for j in range(2):
        rows = jnp.dot(hid[j], bas[j], preferred_element_type=jnp.float32).reshape(NZ, PAIR, R)
        pz[:, j] = jnp.concatenate([rows[:, :, :LANE], rows[:, :, LANE:]], axis=1).astype(jnp.bfloat16)
    landed(cx, load_sem.at[0])

    pl.semaphore_wait(barrier, 7 * (NX - 1) + 1 + NZ - 1 + HALF)

    for o in range(1, NX):
        tx, ty = lax.rem(x + o, NX), lax.rem(y + o, NX)
        push(aux.at[ty], arx.at[x, y, k], a_send.at[o], a_recv.at[x, y], (chip(x, ty), ex))
        push(cx.at[tx], crx.at[x, y, k], c_send.at[o], c_recv.at[x, y], (chip(tx, y), ex))
    pltpu.make_async_copy(aux.at[y], arx.at[x, y, k], a_recv.at[x, y]).start()
    pltpu.make_async_copy(cx.at[x], crx.at[x, y, k], c_recv.at[x, y]).start()

    mine = pl.ds(k * 2, 2)

    def reach(d):
        i = HALF - d
        down, up = lax.rem(z - d + NZ, NZ), lax.rem(z + d, NZ)
        push(pz.at[down], prx.at[i, mine], z_send.at[i, 0], prx_sem.at[i, k], (dp, down * 2))
        if d < HALF:
            push(pz.at[up], prx.at[i, mine], z_send.at[i, 1], prx_sem.at[i, k], (dp, up * 2 + 1))

    def reached(d):
        landed(pz.at[0], z_send.at[HALF - d, 0])
        if d < HALF:
            landed(pz.at[0], z_send.at[HALF - d, 1])

    for d in range(HALF, 0, -1):
        reach(d)

    @pl.when(k == 0)
    def _():
        push(pz.at[z], prx.at[0, mine], z_send.at[0, 1], prx_sem.at[0, k], (dp, sibling))

    @pl.when(k == 1)
    def _():
        pltpu.make_async_copy(pz.at[z], prx.at[0, mine], prx_sem.at[0, k]).start()

    def share_slots(sx, sy):
        push(arx.at[sx, sy, k], arx.at[sx, sy, k], sa_send.at[sx, sy], sa_recv.at[sx, sy], (dp, sibling))

    def share_columns(sx, sy):
        push(crx.at[sx, sy, k], crx.at[sx, sy, k], sc_send.at[sx, sy], sc_recv.at[sx, sy], (dp, sibling))

    def forward(o):
        sy = lax.rem(y - o + NX, NX)
        landed(arx.at[x, sy, k], a_recv.at[x, sy])
        for t in range(1, NX):
            push(arx.at[x, sy, k], arx.at[x, sy, k], ax_send.at[o, t], a_recv.at[x, sy], (chip(lax.rem(x + t, NX), y), ex))
        share_slots(x, sy)
        sx = lax.rem(x - o + NX, NX)
        landed(crx.at[sx, y, k], c_recv.at[sx, y])
        for t in (1, NX - 1):
            push(crx.at[sx, y, k], crx.at[sx, y, k], cy_send.at[o, t], c_recv.at[sx, y], (chip(x, lax.rem(y + t, NX)), ex))
        share_columns(sx, y)

    def spread_y(i):
        for core in range(2):
            landed(prx.at[i, pl.ds(core * 2, 2)], prx_sem.at[i, core])
        for t in range(1, NX):
            ty = lax.rem(y + t, NX)
            push(prx.at[i, ty], pg.at[i, x, y], p1_send.at[i, t], p1_recv.at[i, y], (chip(x, ty), ex))
        pltpu.make_async_copy(prx.at[i, y], pg.at[i, x, y], p1_recv.at[i, y]).start()

    def spread_x(i):
        for sy in range(NX):
            landed(pg.at[i, x, sy], p1_recv.at[i, sy])
        for t in range(1, NX):
            push(pg.at[i, x], pg.at[i, x], p2_send.at[i, t], p2_recv.at[i, x], (chip(lax.rem(x + t, NX), y), ex))

    def receive(o, t):
        sx, sy = lax.rem(x - t + NX, NX), lax.rem(y - o + NX, NX)
        landed(arx.at[sx, sy, k], a_recv.at[sx, sy])
        share_slots(sx, sy)
        sx, sy = lax.rem(x - o + NX, NX), lax.rem(y - t + NX, NX)
        landed(crx.at[sx, sy, k], c_recv.at[sx, sy])
        if t == (1 if o % 2 == 0 else NX - 1):
            over = chip(x, lax.rem(y + t, NX))
            push(crx.at[sx, sy, k], crx.at[sx, sy, k], cy_send.at[o, 2], c_recv.at[sx, sy], (over, ex))
        share_columns(sx, sy)

    first = pl.multiple_of((1 - k) * HALF, HALF)
    slot = lax.broadcasted_iota(jnp.int32, (HALF, PAIR, 2 * TOK), 1).astype(jnp.float32)

    def rows_of(sx, sy):
        landed(arx.at[sx, sy, 1 - k], sa_recv.at[sx, sy])
        landed(crx.at[sx, sy, 1 - k], sc_recv.at[sx, sy])
        place = jnp.concatenate([arx[sx, sy, c, 0, pl.ds(first, HALF), :] for c in range(2)], axis=1)
        gate = jnp.concatenate([arx[sx, sy, c, 1, pl.ds(first, HALF), :] for c in range(2)], axis=1)
        here = slot == place[:, None, :]
        weight = jnp.sum(jnp.where(here, gate[:, None, :], 0.0), axis=2, keepdims=True)
        pick = jnp.where(here, 1.0, 0.0).reshape(HALF * PAIR, 2 * TOK).astype(jnp.bfloat16)
        rows = jnp.dot(pick, crx[sx, sy].reshape(2 * TOK, WIDE), preferred_element_type=jnp.float32)
        return rows.reshape(HALF, PAIR, WIDE) * weight

    def build(pair, carry):
        sx, sy = pair // 2, 2 * lax.rem(pair, 2)
        both = jnp.concatenate([rows_of(sx, sy), rows_of(sx, sy + 1)], axis=1)
        tab[:, pair] = both.astype(jnp.bfloat16)
        return carry

    todo = [(0, 1), (0, 3)]
    for o in range(1, NX):
        todo += [(o, 1), (o, 3), (o - 1, 2)]
    todo.append((NX - 1, 2))

    def take(n):
        for _ in range(n):
            receive(*todo.pop(0))

    def more(d):
        reached(d + 3)
        reach(d)

    onward = lax.rem(z + ahead + NZ, NZ) * 2 + k

    def turn(i):
        for t in range(1, NX):
            sx = lax.rem(x + t, NX)
            landed(pg.at[i, sx], p2_recv.at[i, sx])
        got = pg[i].astype(jnp.float32).reshape(PLANE, 2, PAIR, LANE)
        for h in range(2):
            pt[i, h * LANE : (h + 1) * LANE, :] = got[:, h].reshape(PLANE * PAIR, LANE).T.astype(jnp.bfloat16)

    def block(i, b):
        table = tab[jnp.where(k == 0, HALF - 1 - i, (i + HALF - 1) % HALF), :, :, b * LANE : (b + 1) * LANE]
        return jnp.dot(pt[i], table.reshape(PLANE * PAIR, LANE), preferred_element_type=jnp.float32)

    def arrived(i, b):
        landed(rxs.at[i, b], s_recv.at[i, b])
        landed(rxq.at[i, b], q_recv.at[i, b])
        return rxq[i, b].astype(jnp.int32).astype(jnp.float32) * rxs[i, b, 0:1, :]

    def code(value, i, b):
        most = jnp.maximum(jnp.max(jnp.abs(value), axis=0, keepdims=True), 1e-33)
        txq[i, b] = jnp.round(value * (FULL / most)).astype(jnp.int32).astype(jnp.int16)
        txs[i, b] = jnp.broadcast_to(most * (1.0 / FULL), (8, LANE))

    def push_on(i, b):
        push(txs.at[i, b], rxs.at[i + 1, b], s_send.at[i, b], s_recv.at[i + 1, b], (dp, onward))
        push(txq.at[i, b], rxq.at[i + 1, b], q_send.at[i, b], q_recv.at[i + 1, b], (dp, onward))

    owner_core = y // 2
    part = lax.rem(y, 2)

    def here(b):
        return (y == b) & (owner_core == k)

    def push_owner(i, b, source, plane):
        owner = (b * NX + x, plane * 2 + owner_core)
        push(txs.at[i, b], fins.at[source, part], s_send.at[i, b], fs_recv.at[source, part], owner)
        push(txq.at[i, b], finq.at[source, part], q_send.at[i, b], fq_recv.at[source, part], owner)

    def hop(i):
        turn(i)
        for b in range(NX):
            own[b] = block(i, b)
        for b in range(NX):
            value = own[b]
            if i == 0:
                code(value, 0, b)

                @pl.when(k == 0)
                def _():
                    push_on(0, b)

                @pl.when((k == 1) & here(b))
                def _():
                    pltpu.make_async_copy(txs.at[0, b], fins.at[2, part], fs_recv.at[2, part]).start()
                    pltpu.make_async_copy(txq.at[0, b], finq.at[2, part], fq_recv.at[2, part]).start()

                @pl.when((k == 1) & jnp.logical_not(here(b)))
                def _():
                    push_owner(0, b, 2, z)

            elif i == 1:
                @pl.when(k == 0)
                def _():
                    own[b] += arrived(1, b)

                code(own[b], 1, b)
                push_on(1, b)
            else:
                code(value + arrived(i, b), i, b)
                if i < HALF - 1:
                    push_on(i, b)
                else:
                    push_owner(i, b, k, lax.rem(z + ahead + NZ, NZ))

    forward(0)
    forward(1)
    forward(2)
    forward(3)
    take(2)
    spread_y(0)
    take(3)
    spread_y(1)
    take(3)
    spread_x(0)
    spread_x(1)
    take(3)
    spread_y(2)
    spread_y(3)
    spread_y(4)
    take(1)
    spread_x(2)
    spread_y(5)
    spread_x(3)
    spread_y(6)
    spread_x(4)
    spread_y(7)
    lax.fori_loop(0, 4, build, 0)
    spread_x(5)
    lax.fori_loop(4, 8, build, 0)
    hop(0)
    spread_x(6)
    hop(1)
    spread_x(7)
    hop(2)
    hop(3)
    hop(4)
    hop(5)
    hop(6)
    hop(7)

    for j in range(2):
        total = None
        for core in (2, 0, 1):
            landed(fins.at[core, j], fs_recv.at[core, j])
            landed(finq.at[core, j], fq_recv.at[core, j])
            value = finq[core, j].astype(jnp.int32).astype(jnp.float32) * fins[core, j, 0:1, :]
            total = value if total is None else total + value
        out[j] = total

    for d in range(HALF, 0, -1):
        reached(d)

    @pl.when(k == 0)
    def _():
        landed(pz.at[0], z_send.at[0, 1])

    def left(i, carry):
        for t in range(1, NX):
            landed(pz.at[0, 0], p1_send.at[i, t])
            landed(pg.at[i, 0], p2_send.at[i, t])
        return carry

    lax.fori_loop(0, HALF, left, 0)

    def gone(o, carry):
        for t in range(NX):
            landed(aux.at[0], sa_send.at[o, t])
            landed(cx.at[0], sc_send.at[o, t])
        for t in range(1, NX):
            landed(aux.at[0], ax_send.at[o, t])
            landed(cx.at[0], cy_send.at[o, t])

        @pl.when(o > 0)
        def _():
            landed(aux.at[0], a_send.at[o])
            landed(cx.at[0], c_send.at[o])

        return carry

    lax.fori_loop(0, NX, gone, 0)

    def sent(i, carry):
        for b in range(NX):
            landed(txs.at[i, b], s_send.at[i, b])
            landed(txq.at[i, b], q_send.at[i, b])
        return carry

    lax.fori_loop(1, HALF, sent, 0)

    for b in range(NX):

        @pl.when((k == 0) | jnp.logical_not(here(b)))
        def _():
            landed(txs.at[0, b], s_send.at[0, b])
            landed(txq.at[0, b], q_send.at[0, b])


def exchange(cotangent, routes, gates, hidden, basis):
    dma = pltpu.SemaphoreType.DMA
    square = dma((NX, NX))
    return pl.pallas_call(
        kernel,
        out_shape=jax.ShapeDtypeStruct((2, R, LANE), jnp.float32),
        in_specs=[pl.BlockSpec(memory_space=pltpu.HBM)] * 5,
        out_specs=pl.BlockSpec(memory_space=pltpu.VMEM),
        scratch_shapes=[
            pltpu.VMEM(routes.shape, jnp.int32),
            pltpu.VMEM(gates.shape, jnp.float32),
            pltpu.VMEM((NX, TOK, WIDE), jnp.bfloat16),
            pltpu.VMEM((NX, 2, NZ, TOK), jnp.float32),
            pltpu.VMEM(hidden.shape[1:], jnp.bfloat16),
            pltpu.VMEM(basis.shape, jnp.bfloat16),
            pltpu.VMEM((NZ, 2, 2 * PAIR, LANE), jnp.bfloat16),
            dma((5,)),
            pltpu.VMEM((HALF, NX, 2 * PAIR, LANE), jnp.bfloat16),
            pltpu.VMEM((HALF, NX, NX, 2 * PAIR, LANE), jnp.bfloat16),
            pltpu.VMEM((NX, NX, 2, TOK, WIDE), jnp.bfloat16),
            pltpu.VMEM((NX, NX, 2, 2, NZ, TOK), jnp.float32),
            pltpu.VMEM((HALF, PLANE // 2, 2 * PAIR, WIDE), jnp.bfloat16),
            pltpu.VMEM((HALF, R, PLANE * PAIR), jnp.bfloat16),
            pltpu.VMEM((NX, R, LANE), jnp.float32),
            pltpu.VMEM((HALF + 1, NX, R, LANE), jnp.int16),
            pltpu.VMEM((HALF + 1, NX, 8, LANE), jnp.float32),
            pltpu.VMEM((HALF + 1, NX, R, LANE), jnp.int16),
            pltpu.VMEM((HALF + 1, NX, 8, LANE), jnp.float32),
            pltpu.VMEM((3, 2, R, LANE), jnp.int16),
            pltpu.VMEM((3, 2, 8, LANE), jnp.float32),
            dma((HALF, 2)),
            dma((HALF, 2)),
            dma((NX,)), dma((NX,)), square, square, square, square,
            square, square, square, square,
            dma((HALF, NX)), dma((HALF, NX)), dma((HALF, NX)), dma((HALF, NX)),
            dma((HALF, NX)), dma((HALF, NX)),
            dma((HALF + 1, NX)), dma((HALF + 1, NX)),
            dma((3, 2)), dma((3, 2)),
        ],
        compiler_params=pltpu.CompilerParams(
            collective_id=0, has_side_effects=True, vmem_limit_bytes=56 * 1024 * 1024
        ),
        cost_estimate=pl.CostEstimate(flops=2_700_000_000, bytes_accessed=4_000_000, transcendentals=0),
    )(cotangent, routes, gates, hidden, basis)


def body(cotangent, routes, gate_weights, hidden, galore_basis, moment, second):
    gradient = exchange(cotangent, routes.T, gate_weights.T, hidden, galore_basis)
    new_moment = beta_one * moment + (1.0 - beta_one) * gradient
    new_second = beta_two * second + (1.0 - beta_two) * gradient * gradient
    update = (
        new_moment
        / (1.0 - beta_one**STEP)
        / (jnp.sqrt(new_second / (1.0 - beta_two**STEP)) + epsilon)
    )
    return (new_moment, new_second, update)


def solution(mesh):
    placed = (
        P(("dp", "expert"), None),
        P(("dp", "expert"), None),
        P(("dp", "expert"), None),
        P("dp", "expert", None, None),
        P("expert", None, None),
        P("expert", None, "dp"),
        P("expert", None, "dp"),
    )
    return jax.shard_map(
        body,
        mesh=mesh,
        in_specs=placed,
        out_specs=(P("expert", None, "dp"), P("expert", None, "dp"), P("expert", None, "dp")),
        check_vma=False,
    )
```
